32 devices in a mesh: occ: 8 (over y, x, core), vir: 4 (over z).
Axes of the slice: x: 2, y: 2, z: 4, core: 2. Of those that a mesh axis runs over, the one named last changes fastest.
Arguments:
- amplitudes: float32 [1024, 2048], P('occ'), may hold values from -6 to 6
- amp_cols: int32 [8, 32], P('occ'), may hold values from 0 to 63, all different within a row
- integrals: float32 [4, 8, 64, 1024], P('vir', 'occ'), may hold values from -0.25 to 0.25
- int_rows: int32 [4, 8, 16], P('vir', 'occ'), may hold values from 0 to 63
- int_cols: int32 [4, 8, 16], P('vir', 'occ'), may hold values from 0 to 31
Outputs:
- ladder: float32 [1024, 2048], P(('occ', 'vir'))
The draws below stay inside these ranges and needn't reach their ends.
Inputs may be any that keep to these rules, and one draw needn't show every extreme that they name: `amp_cols`: each row names 32 different contracted tiles, and every tile is named by some row. `int_rows`: tiles may repeat; repeated tiles add.
All inputs are finite; a program needn't handle non-finite values.
Results may differ from the reference program's by a relative error of at most 0.0003.
Values sent between devices are 32-bit elements; how exact they have to be, the bound alone decides.
No kernel may reach another device: no remote copies, remote signals or barrier semaphores. Data moves between devices by JAX's collectives and lax.ppermute only.
A program may use at most 128 MiB of HBM per device.

```python
import jax
import jax.numpy as jnp
from jax import lax

TILE = 64
PAIR_DEV = 128
NA = 32
NV = 16
AB_TILES = 32
CD_TILES = 64
PAIRS = 1024
N_OCC = 8
N_VIR = 4


def with_ends(values, rng, smallest, largest):
    longest = values.shape.index(max(values.shape))
    spots = []
    for shift in (0, 1):
        where = [jax.random.randint(jax.random.fold_in(rng, axis), (), 0, length) for axis, length in enumerate(values.shape)]
        where[longest] = (where[longest] + shift) % values.shape[longest]
        spots.append(tuple(where))
    return values.at[spots[0]].set(smallest).at[spots[1]].set(largest)


def block_levels(key, dims, split, least, top_value):
    factor_of, own = 1.0, jax.random.fold_in(key, 6)
    for dim, shards_of in split:
        heights = jnp.exp(jax.random.uniform(jax.random.fold_in(own, dim), (shards_of,), jnp.float32, least / len(split), top_value / len(split)))
        factor_of = factor_of * jnp.repeat(heights, dims[dim] // shards_of).reshape([-1 if axis == dim else 1 for axis in range(len(dims))])
    return factor_of


def picks_of(key, rows, amount, top, lift):
    order = jax.random.permutation(jax.random.fold_in(key, 1), amount)
    favour = order
    for power in range(3):
        favour = favour * favour // amount
    favour = favour * lift // amount
    chance = jax.random.randint(jax.random.fold_in(key, 2), (rows, amount), 0, 4096) + favour
    fixed_rows = jax.random.permutation(jax.random.fold_in(key, 3), rows)[jnp.arange(amount) % rows]
    chance = jnp.where(jnp.arange(rows)[:, None] == fixed_rows[None, :], 1 << 14, chance)
    merit = chance * amount + jnp.arange(amount)
    return lax.top_k(merit.astype(jnp.int32), top)[1].astype(jnp.int32)


def scatter_about(key, shape, width, bound, cuts=(), kind=jnp.bfloat16):
    level = block_levels(key, shape, cuts, -0.22, 0.18) if cuts else 1.0
    values = jax.random.normal(key, shape, jnp.float32) * width * level
    return jnp.minimum(jnp.maximum(values, -bound), bound).astype(kind)


def setup_inputs(seed: int = 0) -> dict:
    key_list = jax.random.split(jax.random.key(seed), 6)
    return {
        "amplitudes": scatter_about(key_list[0], (PAIRS, NA * TILE), 1.0, 6.0, ((0, 8),), jnp.float32),
        "amp_cols": picks_of(key_list[1], N_OCC, CD_TILES, NA, 0),
        "integrals": scatter_about(key_list[2], (N_VIR, N_OCC, TILE, NV * TILE), (TILE * max(1, N_VIR * N_OCC * NV // (2 * AB_TILES))) ** -0.5, 0.25, ((0, 4), (1, 8)), jnp.float32),
        "int_rows": with_ends(jax.random.randint(key_list[3], (N_VIR, N_OCC, NV), 0, CD_TILES), jax.random.fold_in(key_list[3], 1), 0, CD_TILES - 1).astype(jnp.int32),
        "int_cols": with_ends(jax.random.randint(key_list[4], (N_VIR, N_OCC, NV), 0, AB_TILES), jax.random.fold_in(key_list[4], 1), 0, AB_TILES - 1).astype(jnp.int32),
    }


def reference(amplitudes, amp_cols, integrals, int_rows, int_cols):
    tile_count = N_VIR * N_OCC * NV
    tile_list = integrals.reshape(N_VIR * N_OCC, TILE, NV, TILE).transpose(0, 2, 1, 3).reshape(tile_count, TILE, TILE)
    row_ids = int_rows.reshape(tile_count).astype(jnp.int32)
    col_ids = int_cols.reshape(tile_count).astype(jnp.int32)
    slab_list = amplitudes.reshape(N_OCC, PAIR_DEV, NA * TILE)
    slot_ids = jnp.arange(NA, dtype=jnp.int32)

    def one_slab(entry_pair):
        slab_rows, slot_names = entry_pair
        matches = row_ids[:, None] == slot_names[None, :]
        is_hit = jnp.any(matches, axis=1)
        slot_of = jnp.sum(jnp.where(matches, slot_ids[None, :], 0), axis=1).astype(jnp.int32)
        placed = jnp.where(is_hit[:, None, None], tile_list, jnp.zeros_like(tile_list))
        selected = jnp.zeros((NA, TILE, AB_TILES, TILE), jnp.float32)
        selected = selected.at[slot_of, :, col_ids, :].add(placed)
        return jnp.dot(slab_rows, selected.reshape(NA * TILE, AB_TILES * TILE), precision=lax.Precision.HIGHEST, preferred_element_type=jnp.float32)

    result = lax.map(one_slab, (slab_list, amp_cols))
    return result.reshape(PAIRS, AB_TILES * TILE)
```

```python
import functools

import jax
import jax.numpy as jnp
from jax import lax
from jax.experimental import pallas as pl
from jax.experimental.pallas import tpu as pltpu
from jax.sharding import PartitionSpec as P

AB_TILES = 32
CD_TILES = 64
LANES = 128
UNROLL = 4


def pack_kernel(tiles_ref, rows_ref, cols_ref, out_ref):
    side, width = tiles_ref.shape
    groups = width // LANES
    for g in range(groups):
        out_ref[g * side : (g + 1) * side, :] = tiles_ref[:, g * LANES : (g + 1) * LANES]
    count = rows_ref.shape[1]
    base = groups * side
    out_ref[base : base + 8, :] = jnp.zeros((8, LANES), jnp.float32)
    out_ref[base : base + 1, :count] = rows_ref[...].astype(jnp.float32)
    out_ref[base + 1 : base + 2, :count] = cols_ref[...].astype(jnp.float32)


def pack(tiles, rows, cols):
    side, width = tiles.shape
    return pl.pallas_call(
        pack_kernel,
        out_shape=jax.ShapeDtypeStruct((width // LANES * side + 8, LANES), jnp.float32),
        name="pack",
    )(tiles, rows, cols)


def split(value):
    high = value.astype(jnp.bfloat16)
    low = (value - high.astype(jnp.float32)).astype(jnp.bfloat16)
    return high, low


def product_kernel(n_in, n_out, side, count, names_ref, blocks_ref, amp_ref, *refs):
    packs = refs[:n_in]
    outs = refs[n_in : n_in + n_out]
    tiles, ids, three, total, slot_of, entry, sems = refs[n_in + n_out :]
    body = packs[0].shape[0] - 8
    copies = []
    for j in range(n_in):
        id_copy = pltpu.make_async_copy(packs[j].at[pl.ds(body, 8)], ids.at[j], sems.at[j, 0])
        id_copy.start()
        tile_copy = pltpu.make_async_copy(
            packs[j].at[pl.ds(0, body)], tiles.at[pl.ds(j * body, body)], sems.at[j, 1]
        )
        tile_copy.start()
        copies.append((id_copy, tile_copy))

    slots = names_ref.shape[1]

    @pl.loop(0, CD_TILES)
    def _(r):
        slot_of[r] = -1

    @pl.loop(0, slots)
    def _(s):
        slot_of[names_ref[0, s]] = s

    lane = lax.broadcasted_iota(jnp.int32, (1, LANES), 1)
    left = lane < side
    for g in range(amp_ref.shape[1] // LANES):
        both = amp_ref[:, g * LANES : (g + 1) * LANES]
        high = both.astype(jnp.bfloat16).astype(jnp.float32)
        low = both - high
        high_turned = pltpu.roll(high, side, 1)
        low_turned = pltpu.roll(low, side, 1)
        three[2 * g, :, :LANES] = jnp.where(left, high, low_turned).astype(jnp.bfloat16)
        three[2 * g, :, LANES:] = high[:, :side].astype(jnp.bfloat16)
        three[2 * g + 1, :, :LANES] = jnp.where(left, high_turned, low).astype(jnp.bfloat16)
        three[2 * g + 1, :, LANES:] = high_turned[:, :side].astype(jnp.bfloat16)

    total[...] = jnp.zeros_like(total)

    for id_copy, tile_copy in copies:
        id_copy.wait()

    found = 0
    for j in range(n_in):
        for t in range(count):
            row = ids[j, 0, t].astype(jnp.int32)
            col = ids[j, 1, t].astype(jnp.int32)
            slot = slot_of[row]
            entry[found, 0] = slot
            entry[found, 1] = col
            entry[found, 2] = (j * count + t) // 2 * side
            entry[found, 3] = t % 2
            found = found + (slot >= 0).astype(jnp.int32)
    for k in range(UNROLL):
        entry[found + k, 0] = 0
        entry[found + k, 1] = -2
        entry[found + k, 2] = 0
        entry[found + k, 3] = 0
    for id_copy, tile_copy in copies:
        tile_copy.wait()

    @pl.loop(0, (found + UNROLL - 1) // UNROLL)
    def _(step):
        products = []
        for k in range(UNROLL):
            n = step * UNROLL + k
            slot, col, base, half = (entry[n, f] for f in range(4))
            goal = lax.rem(col + 2, 2)
            pair = tiles[pl.ds(pl.multiple_of(base, side), side), :]
            turned = jnp.where(half == goal, pair, pltpu.roll(pair, side, 1))
            keep = (lane >= goal * side) & (lane < goal * side + side) & (col >= 0)
            high, low = split(jnp.where(keep, turned, 0.0))
            weights = jnp.concatenate([high, high, low], axis=0)
            products.append(
                (
                    jnp.maximum(col, 0) // 2,
                    jnp.dot(three[slot], weights, preferred_element_type=jnp.float32),
                )
            )
        for group, product in products:
            total[group] += product

    for b, out_ref in enumerate(outs):
        height = out_ref.shape[0]
        base = pl.multiple_of(blocks_ref[b] * height, height)
        for g in range(total.shape[0]):
            out_ref[:, g * LANES : (g + 1) * LANES] = total[g, pl.ds(base, height), :]


def products(names, blocks, amplitudes, packs, side, count, n_out):
    rows, slots = amplitudes.shape[0], names.shape[1]
    n_in = len(packs)
    body = packs[0].shape[0] - 8
    groups = AB_TILES * side // LANES
    smem = pl.BlockSpec(memory_space=pltpu.SMEM)
    vmem = pl.BlockSpec(memory_space=pltpu.VMEM)
    block = jax.ShapeDtypeStruct((rows // n_out, AB_TILES * side), jnp.float32)
    return pl.pallas_call(
        functools.partial(product_kernel, n_in, n_out, side, count),
        out_shape=[block] * n_out,
        in_specs=[smem, smem, vmem] + [pl.BlockSpec(memory_space=pl.ANY)] * n_in,
        out_specs=[vmem] * n_out,
        scratch_shapes=[
            pltpu.VMEM((n_in * body, LANES), jnp.float32),
            pltpu.SMEM((n_in, 8, LANES), jnp.float32),
            pltpu.VMEM((slots, rows, 3 * side), jnp.bfloat16),
            pltpu.VMEM((groups, rows, LANES), jnp.float32),
            pltpu.SMEM((CD_TILES,), jnp.int32),
            pltpu.SMEM((n_in * count + UNROLL, 4), jnp.int32),
            pltpu.SemaphoreType.DMA((n_in, 2)),
        ],
        compiler_params=pltpu.CompilerParams(vmem_limit_bytes=40 * 1024 * 1024),
        name="products",
    )(names, blocks, amplitudes, *packs)


def local(n_occ, n_vir, amplitudes, amp_cols, integrals, int_rows, int_cols):
    side, width = integrals.shape[2:]
    count = width // side
    own = pack(
        integrals.reshape(side, width),
        int_rows.reshape(1, count),
        int_cols.reshape(1, count),
    )

    def swap(value, mask):
        return lax.ppermute(value, "occ", [(i, i ^ mask) for i in range(n_occ)])

    def along(value, pairs):
        return lax.ppermute(value, "vir", pairs)

    if n_occ == 8:
        first, second, third = swap(own, 2), swap(own, 4), swap(own, 6)
        mine = [own, first, second, third]
        packs = mine + [swap(value, 1) for value in mine]
    else:
        everyone = lax.all_gather(own, "occ", axis=0)
        packs = [everyone[i] for i in range(n_occ)]

    place = lax.axis_index("vir")
    if n_vir == 4:
        table = jnp.array([[3, 1, 2, 0], [0, 2, 3, 1], [3, 1, 0, 2], [0, 2, 1, 3]], jnp.int32)
        near, mid, far, mine = products(
            amp_cols, table[place], amplitudes, packs, side, count, n_vir
        )
        at_end = (place == 0) | (place == 3)
        near = along(near, [(0, 1), (1, 0), (2, 3), (3, 2)])
        middle = along(mid, [(1, 2), (2, 1)])
        far = far + jnp.where(at_end, 0.0, near)
        far = along(far, [(0, 2), (1, 3), (2, 0), (3, 1)])
        outer = along(mid, [(0, 1), (3, 2)])
        return mine + jnp.where(at_end, near, 0.0) + middle + far + outer
    (whole,) = products(amp_cols, jnp.zeros((1,), jnp.int32), amplitudes, packs, side, count, 1)
    return lax.psum_scatter(whole, "vir", scatter_dimension=0, tiled=True)


def solution(mesh):
    return jax.shard_map(
        functools.partial(local, mesh.shape["occ"], mesh.shape["vir"]),
        mesh=mesh,
        in_specs=(
            P("occ", None),
            P("occ", None),
            P("vir", "occ", None, None),
            P("vir", "occ", None),
            P("vir", "occ", None),
        ),
        out_specs=P(("occ", "vir"), None),
        check_vma=False,
    )
```

```python
import functools

import jax
import jax.numpy as jnp
from jax import lax
from jax.experimental import pallas as pl
from jax.experimental.pallas import tpu as pltpu
from jax.sharding import PartitionSpec as P

AB_TILES = 32
LANES = 128
UNROLL = 8
PIECES = 2
HBM = pl.BlockSpec(memory_space=pltpu.HBM)
SMEM = pl.BlockSpec(memory_space=pltpu.SMEM)
VMEM = pl.BlockSpec(memory_space=pltpu.VMEM)
PARAMS = pltpu.CompilerParams(vmem_limit_bytes=8 * 1024 * 1024)


def in_vmem(value):
    return pltpu.with_memory_space_constraint(value, pltpu.VMEM)


def in_hbm(value):
    return pltpu.with_memory_space_constraint(value, pltpu.HBM)


def together(*values):
    return lax.optimization_barrier(values)


def pack_kernel(tiles_ref, rows_ref, cols_ref, *refs):
    outs, numbers, sems = refs[:-2], refs[-2], refs[-1]
    side, width = tiles_ref.shape
    count = rows_ref.shape[1] // len(outs)
    groups = width // LANES // len(outs)
    base = groups * side
    copies = [
        pltpu.make_async_copy(rows_ref, numbers.at[0], sems.at[0]),
        pltpu.make_async_copy(cols_ref, numbers.at[1], sems.at[1]),
    ]
    for p, out_ref in enumerate(outs):
        for g in range(groups):
            n = p * groups + g
            copies.append(
                pltpu.make_async_copy(
                    tiles_ref.at[:, pl.ds(n * LANES, LANES)],
                    out_ref.at[pl.ds(g * side, side)],
                    sems.at[2 + n],
                )
            )
    for copy in copies:
        copy.start()
    for out_ref in outs:
        out_ref[base : base + 8, :] = jnp.zeros((8, LANES), jnp.float32)
    for copy in copies[:2]:
        copy.wait()
    for p, out_ref in enumerate(outs):
        for k in range(2):
            values = numbers[k][:, p * count : (p + 1) * count]
            out_ref[base + k : base + k + 1, :count] = values.astype(jnp.float32)
    for copy in copies[2:]:
        copy.wait()


def pack(tiles, rows, cols, parts):
    side, width = tiles.shape
    groups = width // LANES
    return pl.pallas_call(
        pack_kernel,
        out_shape=[pltpu.VMEM((groups // parts * side + 8, LANES), jnp.float32)] * parts,
        in_specs=[HBM] * 3,
        out_specs=[VMEM] * parts,
        scratch_shapes=[
            pltpu.VMEM((2, 1, rows.shape[1]), jnp.int32),
            pltpu.SemaphoreType.DMA((2 + groups,)),
        ],
        compiler_params=PARAMS,
        name="pack",
    )(in_hbm(tiles), in_hbm(rows), in_hbm(cols))


def split(value):
    high = value.astype(jnp.bfloat16)
    low = (value - high.astype(jnp.float32)).astype(jnp.bfloat16)
    return high, low


def prepare_kernel(n_blocks, side, place_ref, names_in, amp_ref, three_ref, names_out, names_ref, amps, sems):
    place = place_ref[0]
    rows = amp_ref.shape[0]
    height = rows // n_blocks
    names_copy = pltpu.make_async_copy(names_in, names_ref, sems.at[n_blocks])
    names_copy.start()
    copies = []
    for b in range(n_blocks):
        source = pl.ds(pl.multiple_of((place ^ b) * height, height), height)
        copy = pltpu.make_async_copy(amp_ref.at[source], amps.at[b], sems.at[b])
        copy.start()
        copies.append(copy)
    names_copy.wait()
    for s in range(names_ref.shape[1]):
        names_out[s : s + 1, :] = jnp.full((1, LANES), names_ref[0, s], jnp.int32)
    lane = lax.broadcasted_iota(jnp.int32, (1, LANES), 1)
    left = lane < side
    for b in range(n_blocks):
        here = slice(b * height, (b + 1) * height)
        copies[b].wait()
        for g in range(amp_ref.shape[1] // LANES):
            both = amps[b, :, g * LANES : (g + 1) * LANES]
            high = both.astype(jnp.bfloat16).astype(jnp.float32)
            low = both - high
            high_turned = pltpu.roll(high, side, 1)
            low_turned = pltpu.roll(low, side, 1)
            three_ref[2 * g, here, :LANES] = jnp.where(left, high, low_turned).astype(jnp.bfloat16)
            three_ref[2 * g, here, LANES:] = high[:, :side].astype(jnp.bfloat16)
            three_ref[2 * g + 1, here, :LANES] = jnp.where(left, high_turned, low).astype(jnp.bfloat16)
            three_ref[2 * g + 1, here, LANES:] = high_turned[:, :side].astype(jnp.bfloat16)


def prepare(place, names, amplitudes, n_blocks):
    rows, width = amplitudes.shape
    slots = names.shape[1]
    side = width // slots
    return pl.pallas_call(
        functools.partial(prepare_kernel, n_blocks, side),
        out_shape=[
            pltpu.VMEM((slots, rows, 3 * side), jnp.bfloat16),
            pltpu.VMEM((slots, LANES), jnp.int32),
        ],
        in_specs=[SMEM, HBM, HBM],
        out_specs=[VMEM, VMEM],
        scratch_shapes=[
            pltpu.SMEM((1, slots), jnp.int32),
            pltpu.VMEM((n_blocks, rows // n_blocks, width), jnp.float32),
            pltpu.SemaphoreType.DMA((n_blocks + 1,)),
        ],
        compiler_params=PARAMS,
        name="prepare",
        cost_estimate=pl.CostEstimate(flops=0, bytes_accessed=0, transcendentals=0),
    )(place, in_hbm(names), in_hbm(amplitudes))


def product_kernel(n_in, n_outs, first, side, count, names_ref, three_ref, *refs):
    packs = refs[:n_in]
    outs = refs[-n_outs - 3 : -3]
    numbers, words, sem = refs[-3:]
    body = packs[0].shape[0] - 8
    slots = names_ref.shape[0]
    slot_id = lax.broadcasted_iota(jnp.int32, (slots, LANES), 0) + 1
    for j in range(n_in):
        rows = packs[j][body : body + 1, :].astype(jnp.int32)
        slot = jnp.sum(jnp.where(names_ref[...] == rows, slot_id, 0), axis=0, keepdims=True)
        cols = packs[j][body + 1 : body + 2, :].astype(jnp.int32)
        numbers[j : j + 1, :] = slot * AB_TILES + cols
    copy = pltpu.make_async_copy(numbers, words, sem)
    copy.start()
    if first:
        for out_ref in outs:
            out_ref[...] = jnp.zeros_like(out_ref)
    copy.wait()

    lane = lax.broadcasted_iota(jnp.int32, (1, LANES), 1)
    tiles = [(j, t) for j in range(n_in) for t in range(count)]
    for start in range(0, len(tiles), UNROLL):
        products = []
        for j, t in tiles[start : start + UNROLL]:
            word = words[j, t]
            col = word & (AB_TILES - 1)
            slot = word // AB_TILES
            goal = col & 1
            pair = packs[j][t // 2 * side : (t // 2 + 1) * side, :]
            turned = jnp.where(goal == t % 2, pair, pltpu.roll(pair, side, 1))
            keep = (lane >= goal * side) & (lane < goal * side + side) & (slot > 0)
            high, low = split(jnp.where(keep, turned, 0.0))
            weights = jnp.concatenate([high, high, low], axis=0)
            values = three_ref[jnp.maximum(slot - 1, 0)]
            products.append(
                (
                    pl.multiple_of(col // 2 * LANES, LANES),
                    jnp.dot(values, weights, preferred_element_type=jnp.float32),
                )
            )
        for column, product in products:
            for b, out_ref in enumerate(outs):
                height = out_ref.shape[0]
                out_ref[:, pl.ds(column, LANES)] += product[b * height : (b + 1) * height]


def accumulate(names, three, packs, totals, n_outs, side, count):
    rows, n_in = three.shape[1], len(packs)
    block = pltpu.VMEM((rows // n_outs, AB_TILES * side), jnp.float32)
    carried = [] if totals is None else [in_vmem(total) for total in totals]
    return pl.pallas_call(
        functools.partial(product_kernel, n_in, n_outs, totals is None, side, count),
        out_shape=[block] * n_outs,
        in_specs=[VMEM] * (2 + n_in + len(carried)),
        out_specs=[VMEM] * n_outs,
        input_output_aliases={2 + n_in + b: b for b in range(len(carried))},
        scratch_shapes=[
            pltpu.VMEM((8, LANES), jnp.int32),
            pltpu.SMEM((8, LANES), jnp.int32),
            pltpu.SemaphoreType.DMA,
        ],
        compiler_params=PARAMS,
        name="products",
        cost_estimate=pl.CostEstimate(flops=0, bytes_accessed=0, transcendentals=0),
    )(in_vmem(names), in_vmem(three), *map(in_vmem, packs), *carried)


def add_kernel(carried_ref, more_ref, out_ref):
    out_ref[...] = carried_ref[...] + more_ref[...]


def added(carried, more):
    return pl.pallas_call(
        add_kernel,
        out_shape=pltpu.VMEM(carried.shape, carried.dtype),
        in_specs=[VMEM, VMEM],
        out_specs=VMEM,
        input_output_aliases={0: 0},
        compiler_params=PARAMS,
        name="added",
    )(in_vmem(carried), in_vmem(more))


def local(n_occ, n_vir, amplitudes, amp_cols, integrals, int_rows, int_cols):
    side, width = integrals.shape[2:]
    count = width // side
    place = lax.axis_index("vir").astype(jnp.int32).reshape(1)

    def swap(value, mask):
        return lax.ppermute(value, "occ", [(i, i ^ mask) for i in range(n_occ)])

    def along(value, mask):
        return lax.ppermute(value, "vir", [(i, i ^ mask) for i in range(n_vir)])

    low, high = pack(
        integrals.reshape(side, width),
        int_rows.reshape(1, count),
        int_cols.reshape(1, count),
        2,
    )

    def add(packs, blocks):
        return accumulate(names, three, packs, blocks, PIECES * n_vir, side, count // 2)

    if n_occ == 8:
        x_low, y_high, x_high, y_low = swap(low, 2), swap(high, 4), swap(high, 2), swap(low, 4)
        close = [swap(low, 1), swap(high, 1)]
        three, names = prepare(place, amp_cols, amplitudes, n_vir)
        blocks = add([low, high], None)
        x_low, y_high, blocks = together(x_low, y_high, blocks)
        far_low, far_high = swap(x_low, 4), swap(y_high, 2)
        turned = [swap(x_low, 1), swap(y_high, 1)]
        blocks = add([x_low, y_high] + close, blocks)
        x_high, y_low, blocks = together(x_high, y_low, blocks)
        later = [swap(x_high, 1), swap(y_low, 1)]
        blocks = add([x_high, y_low] + turned, blocks)
        far_low, far_high, blocks = together(far_low, far_high, blocks)
        last = [swap(far_low, 1), swap(far_high, 1)]
        blocks = add([far_low, far_high] + later, blocks)
        blocks = list(add(last, blocks))
    else:
        three, names = prepare(place, amp_cols, amplitudes, n_vir)
        blocks = add([low, high], None)
        for mask in range(1, n_occ):
            blocks = add([swap(low, mask), swap(high, mask)], blocks)
        blocks = list(blocks)

    blocks = [blocks[r * PIECES : (r + 1) * PIECES] for r in range(n_vir)]
    bit = 1
    while bit < n_vir:
        sent = range(n_vir - bit, 0, -2 * bit)
        got = {r: [along(piece, bit) for piece in blocks[r]] for r in sent}
        for r in sent:
            blocks[r ^ bit] = [added(old, new) for old, new in zip(blocks[r ^ bit], got[r])]
        bit *= 2
    return jnp.concatenate(blocks[0], axis=0)


def solution(mesh):
    return jax.shard_map(
        functools.partial(local, mesh.shape["occ"], mesh.shape["vir"]),
        mesh=mesh,
        in_specs=(
            P("occ", None),
            P("occ", None),
            P("vir", "occ", None, None),
            P("vir", "occ", None),
            P("vir", "occ", None),
        ),
        out_specs=P(("occ", "vir"), None),
        check_vma=False,
    )
```

```python
import functools

import jax
import jax.numpy as jnp
from jax import lax
from jax.experimental import pallas as pl
from jax.experimental.pallas import tpu as pltpu
from jax.sharding import PartitionSpec as P

AB_TILES = 32
LANES = 128
UNROLL = 8
PARTS = 1
HBM = pl.BlockSpec(memory_space=pltpu.HBM)
SMEM = pl.BlockSpec(memory_space=pltpu.SMEM)
VMEM = pl.BlockSpec(memory_space=pltpu.VMEM)
PARAMS = pltpu.CompilerParams(vmem_limit_bytes=8 * 1024 * 1024)


def in_vmem(value):
    return pltpu.with_memory_space_constraint(value, pltpu.VMEM)


def in_hbm(value):
    return pltpu.with_memory_space_constraint(value, pltpu.HBM)


def together(*values):
    return lax.optimization_barrier(values)


def pack_kernel(tiles_ref, rows_ref, cols_ref, out_ref, numbers, sems):
    side, width = tiles_ref.shape
    count = rows_ref.shape[1] // PARTS
    groups = width // LANES // PARTS
    rows = groups * side + 8
    copies = [
        pltpu.make_async_copy(rows_ref, numbers.at[0], sems.at[0]),
        pltpu.make_async_copy(cols_ref, numbers.at[1], sems.at[1]),
    ]
    for n in range(PARTS * groups):
        copies.append(
            pltpu.make_async_copy(
                tiles_ref.at[:, pl.ds(n * LANES, LANES)],
                out_ref.at[pl.ds(n // groups * rows + n % groups * side, side)],
                sems.at[2 + n],
            )
        )
    for copy in copies:
        copy.start()
    for p in range(PARTS):
        out_ref[(p + 1) * rows - 8 : (p + 1) * rows, :] = jnp.zeros((8, LANES), jnp.float32)
    for copy in copies[:2]:
        copy.wait()
    for p in range(PARTS):
        for k in range(2):
            place = (p + 1) * rows - 8 + k
            values = numbers[k][:, p * count : (p + 1) * count]
            out_ref[place : place + 1, :count] = values.astype(jnp.float32)
    for copy in copies[2:]:
        copy.wait()


def pack(tiles, rows, cols):
    side, width = tiles.shape
    groups = width // LANES
    return pl.pallas_call(
        pack_kernel,
        out_shape=pltpu.VMEM((groups * side + PARTS * 8, LANES), jnp.float32),
        in_specs=[HBM] * 3,
        out_specs=VMEM,
        scratch_shapes=[
            pltpu.VMEM((2, 1, rows.shape[1]), jnp.int32),
            pltpu.SemaphoreType.DMA((2 + groups,)),
        ],
        compiler_params=PARAMS,
        name="pack",
    )(in_hbm(tiles), in_hbm(rows), in_hbm(cols))


def split(value):
    high = value.astype(jnp.bfloat16)
    low = (value - high.astype(jnp.float32)).astype(jnp.bfloat16)
    return high, low


def prepare_kernel(n_blocks, side, place_ref, names_in, amp_ref, three_ref, names_out, names_ref, amps, sems):
    place = place_ref[0]
    rows = amp_ref.shape[0]
    height = rows // n_blocks
    names_copy = pltpu.make_async_copy(names_in, names_ref, sems.at[n_blocks])
    names_copy.start()
    copies = []
    for b in range(n_blocks):
        source = pl.ds(pl.multiple_of((place ^ b) * height, height), height)
        copy = pltpu.make_async_copy(amp_ref.at[source], amps.at[b], sems.at[b])
        copy.start()
        copies.append(copy)
    names_copy.wait()
    for s in range(names_ref.shape[1]):
        names_out[s : s + 1, :] = jnp.full((1, LANES), names_ref[0, s], jnp.int32)
    lane = lax.broadcasted_iota(jnp.int32, (1, LANES), 1)
    left = lane < side
    for b in range(n_blocks):
        here = slice(b * height, (b + 1) * height)
        copies[b].wait()
        for g in range(amp_ref.shape[1] // LANES):
            both = amps[b, :, g * LANES : (g + 1) * LANES]
            high = both.astype(jnp.bfloat16).astype(jnp.float32)
            low = both - high
            high_turned = pltpu.roll(high, side, 1)
            low_turned = pltpu.roll(low, side, 1)
            three_ref[2 * g, here, :LANES] = jnp.where(left, high, low_turned).astype(jnp.bfloat16)
            three_ref[2 * g, here, LANES:] = high[:, :side].astype(jnp.bfloat16)
            three_ref[2 * g + 1, here, :LANES] = jnp.where(left, high_turned, low).astype(jnp.bfloat16)
            three_ref[2 * g + 1, here, LANES:] = high_turned[:, :side].astype(jnp.bfloat16)


def prepare(place, names, amplitudes, n_blocks):
    rows, width = amplitudes.shape
    slots = names.shape[1]
    side = width // slots
    return pl.pallas_call(
        functools.partial(prepare_kernel, n_blocks, side),
        out_shape=[
            pltpu.VMEM((slots, rows, 3 * side), jnp.bfloat16),
            pltpu.VMEM((slots, LANES), jnp.int32),
        ],
        in_specs=[SMEM, HBM, HBM],
        out_specs=[VMEM, VMEM],
        scratch_shapes=[
            pltpu.SMEM((1, slots), jnp.int32),
            pltpu.VMEM((n_blocks, rows // n_blocks, width), jnp.float32),
            pltpu.SemaphoreType.DMA((n_blocks + 1,)),
        ],
        compiler_params=PARAMS,
        name="prepare",
        cost_estimate=pl.CostEstimate(flops=100, bytes_accessed=100, transcendentals=0),
    )(place, in_hbm(names), in_hbm(amplitudes))


def product_kernel(n_in, n_outs, first, side, count, names_ref, three_ref, *refs):
    packs = refs[:n_in]
    outs = refs[-n_outs - 3 : -3]
    numbers, words, sem = refs[-3:]
    rows = count // 2 * side + 8
    parts = [(pack, base) for pack in packs for base in range(0, pack.shape[0], rows)]
    slots = names_ref.shape[0]
    slot_id = lax.broadcasted_iota(jnp.int32, (slots, LANES), 0) + 1
    for j, (pack, base) in enumerate(parts):
        row = pack[base + rows - 8 : base + rows - 7, :].astype(jnp.int32)
        slot = jnp.sum(jnp.where(names_ref[...] == row, slot_id, 0), axis=0, keepdims=True)
        col = pack[base + rows - 7 : base + rows - 6, :].astype(jnp.int32)
        numbers[j : j + 1, :] = slot * AB_TILES + col
    copy = pltpu.make_async_copy(numbers, words, sem)
    copy.start()
    if first:
        for out_ref in outs:
            out_ref[...] = jnp.zeros_like(out_ref)
    copy.wait()

    lane = lax.broadcasted_iota(jnp.int32, (1, LANES), 1)
    tiles = [(j, t) for j in range(len(parts)) for t in range(count)]
    for start in range(0, len(tiles), UNROLL):
        products = []
        for j, t in tiles[start : start + UNROLL]:
            word = words[j, t]
            col = word & (AB_TILES - 1)
            slot = word // AB_TILES
            goal = col & 1
            pack, base = parts[j]
            pair = pack[base + t // 2 * side : base + (t // 2 + 1) * side, :]
            turned = jnp.where(goal == t % 2, pair, pltpu.roll(pair, side, 1))
            keep = (lane >= goal * side) & (lane < goal * side + side) & (slot > 0)
            high, low = split(jnp.where(keep, turned, 0.0))
            weights = jnp.concatenate([high, high, low], axis=0)
            values = three_ref[jnp.maximum(slot - 1, 0)]
            products.append(
                (
                    pl.multiple_of(col // 2 * LANES, LANES),
                    jnp.dot(values, weights, preferred_element_type=jnp.float32),
                )
            )
        for column, product in products:
            top = 0
            for out_ref in outs:
                height = out_ref.shape[0]
                out_ref[:, pl.ds(column, LANES)] += product[top : top + height]
                top += height


def accumulate(names, three, packs, totals, heights, side, count):
    n_in = len(packs)
    blocks = [pltpu.VMEM((height, AB_TILES * side), jnp.float32) for height in heights]
    carried = [] if totals is None else [in_vmem(total) for total in totals]
    return pl.pallas_call(
        functools.partial(product_kernel, n_in, len(heights), totals is None, side, count),
        out_shape=blocks,
        in_specs=[VMEM] * (2 + n_in + len(carried)),
        out_specs=[VMEM] * len(heights),
        input_output_aliases={2 + n_in + b: b for b in range(len(carried))},
        scratch_shapes=[
            pltpu.VMEM((8, LANES), jnp.int32),
            pltpu.SMEM((8, LANES), jnp.int32),
            pltpu.SemaphoreType.DMA,
        ],
        compiler_params=PARAMS,
        name="products",
        cost_estimate=pl.CostEstimate(flops=100, bytes_accessed=100, transcendentals=0),
    )(in_vmem(names), in_vmem(three), *map(in_vmem, packs), *carried)


def add_kernel(carried_ref, more_ref, out_ref):
    out_ref[...] = carried_ref[...] + more_ref[...]


def added(carried, more):
    return pl.pallas_call(
        add_kernel,
        out_shape=pltpu.VMEM(carried.shape, carried.dtype),
        in_specs=[VMEM, VMEM],
        out_specs=VMEM,
        input_output_aliases={0: 0},
        compiler_params=PARAMS,
        name="added",
        cost_estimate=pl.CostEstimate(flops=0, bytes_accessed=8 << 20, transcendentals=0),
    )(in_vmem(carried), in_vmem(more))


def local(n_occ, n_vir, amplitudes, amp_cols, integrals, int_rows, int_cols):
    side, width = integrals.shape[2:]
    count = width // side
    place = lax.axis_index("vir").astype(jnp.int32).reshape(1)

    def swap(value, mask):
        return lax.ppermute(value, "occ", [(i, i ^ mask) for i in range(n_occ)])

    def along(value, mask):
        return lax.ppermute(value, "vir", [(i, i ^ mask) for i in range(n_vir)])

    own = pack(
        integrals.reshape(side, width),
        int_rows.reshape(1, count),
        int_cols.reshape(1, count),
    )
    height = amplitudes.shape[0] // n_vir
    pieces = [2] * n_vir
    heights = [height // pieces[r] for r in range(n_vir) for _ in range(pieces[r])]

    def add(packs, blocks):
        return accumulate(names, three, packs, blocks, heights, side, count // PARTS)

    if n_occ == 8:
        x, y, far, close = (swap(own, mask) for mask in (2, 4, 6, 1))
        three, names = prepare(place, amp_cols, amplitudes, n_vir)
        blocks = add([own], None)
        x, y, blocks = together(x, y, blocks)
        x_turned, y_turned = swap(x, 1), swap(y, 1)
        blocks = add([x, y, close], blocks)
        far, blocks = together(far, blocks)
        far_turned = swap(far, 1)
        blocks = add([x_turned, y_turned, far], blocks)
        blocks = add([far_turned], blocks)
    else:
        three, names = prepare(place, amp_cols, amplitudes, n_vir)
        blocks = add([own], None)
        for mask in range(1, n_occ):
            blocks = add([swap(own, mask)], blocks)

    blocks = iter(blocks)
    blocks = [[next(blocks) for _ in range(pieces[r])] for r in range(n_vir)]
    bit = 1
    while bit < n_vir:
        for r in range(n_vir - bit, 1, -2 * bit):
            got = [along(piece, bit) for piece in blocks[r]]
            goal = blocks[r ^ bit]
            goal[0] = added(goal[0], got[0])
            if r == 2:
                upper = along(blocks[1][0], 1)
                upper, goal[0], goal[1] = together(upper, goal[0], goal[1])
            goal[1] = added(goal[1], got[1])
        if bit == 1:
            blocks[2][0], *blocks[1] = together(blocks[2][0], *blocks[1])
        bit *= 2
    lower = along(blocks[1][1], 1)
    return jnp.concatenate(blocks[0], axis=0) + jnp.concatenate([upper, lower], axis=0)


def solution(mesh):
    return jax.shard_map(
        functools.partial(local, mesh.shape["occ"], mesh.shape["vir"]),
        mesh=mesh,
        in_specs=(
            P("occ", None),
            P("occ", None),
            P("vir", "occ", None, None),
            P("vir", "occ", None),
            P("vir", "occ", None),
        ),
        out_specs=P(("occ", "vir"), None),
        check_vma=False,
    )
```

```python
import functools

import jax
import jax.numpy as jnp
from jax import lax
from jax.experimental import pallas as pl
from jax.experimental.pallas import tpu as pltpu
from jax.sharding import PartitionSpec as P

AB_TILES = 32
LANES = 128
UNROLL = 8
PARTS = 1
HBM = pl.BlockSpec(memory_space=pltpu.HBM)
SMEM = pl.BlockSpec(memory_space=pltpu.SMEM)
VMEM = pl.BlockSpec(memory_space=pltpu.VMEM)
PARAMS = pltpu.CompilerParams(vmem_limit_bytes=8 * 1024 * 1024)


def in_vmem(value):
    return pltpu.with_memory_space_constraint(value, pltpu.VMEM)


def in_hbm(value):
    return pltpu.with_memory_space_constraint(value, pltpu.HBM)


def together(*values):
    return lax.optimization_barrier(values)


def pack_kernel(tiles_ref, rows_ref, cols_ref, out_ref, numbers, sems):
    side, width = tiles_ref.shape
    count = rows_ref.shape[1] // PARTS
    groups = width // LANES // PARTS
    rows = groups * side + 8
    copies = [
        pltpu.make_async_copy(rows_ref, numbers.at[0], sems.at[0]),
        pltpu.make_async_copy(cols_ref, numbers.at[1], sems.at[1]),
    ]
    for n in range(PARTS * groups):
        copies.append(
            pltpu.make_async_copy(
                tiles_ref.at[:, pl.ds(n * LANES, LANES)],
                out_ref.at[pl.ds(n // groups * rows + n % groups * side, side)],
                sems.at[2 + n],
            )
        )
    for copy in copies:
        copy.start()
    for p in range(PARTS):
        out_ref[(p + 1) * rows - 8 : (p + 1) * rows, :] = jnp.zeros((8, LANES), jnp.float32)
    for copy in copies[:2]:
        copy.wait()
    for p in range(PARTS):
        for k in range(2):
            place = (p + 1) * rows - 8 + k
            values = numbers[k][:, p * count : (p + 1) * count]
            out_ref[place : place + 1, :count] = values.astype(jnp.float32)
    for copy in copies[2:]:
        copy.wait()


def pack(tiles, rows, cols):
    side, width = tiles.shape
    groups = width // LANES
    return pl.pallas_call(
        pack_kernel,
        out_shape=pltpu.VMEM((groups * side + PARTS * 8, LANES), jnp.float32),
        in_specs=[HBM] * 3,
        out_specs=VMEM,
        scratch_shapes=[
            pltpu.VMEM((2, 1, rows.shape[1]), jnp.int32),
            pltpu.SemaphoreType.DMA((2 + groups,)),
        ],
        compiler_params=PARAMS,
        name="pack",
    )(in_hbm(tiles), in_hbm(rows), in_hbm(cols))


def split(value):
    high = value.astype(jnp.bfloat16)
    low = (value - high.astype(jnp.float32)).astype(jnp.bfloat16)
    return high, low


def prepare_kernel(n_blocks, side, place_ref, names_in, amp_ref, three_ref, names_out, names_ref, amps, sems):
    place = place_ref[0]
    rows = amp_ref.shape[0]
    height = rows // n_blocks
    names_copy = pltpu.make_async_copy(names_in, names_ref, sems.at[n_blocks])
    names_copy.start()
    copies = []
    for b in range(n_blocks):
        source = pl.ds(pl.multiple_of((place ^ b) * height, height), height)
        copy = pltpu.make_async_copy(amp_ref.at[source], amps.at[b], sems.at[b])
        copy.start()
        copies.append(copy)
    names_copy.wait()
    for s in range(names_ref.shape[1]):
        names_out[s : s + 1, :] = jnp.full((1, LANES), names_ref[0, s], jnp.int32)
    lane = lax.broadcasted_iota(jnp.int32, (1, LANES), 1)
    left = lane < side
    for b in range(n_blocks):
        here = slice(b * height, (b + 1) * height)
        copies[b].wait()
        for g in range(amp_ref.shape[1] // LANES):
            both = amps[b, :, g * LANES : (g + 1) * LANES]
            high = both.astype(jnp.bfloat16).astype(jnp.float32)
            low = both - high
            high_turned = pltpu.roll(high, side, 1)
            low_turned = pltpu.roll(low, side, 1)
            three_ref[2 * g, here, :LANES] = jnp.where(left, high, low_turned).astype(jnp.bfloat16)
            three_ref[2 * g, here, LANES:] = high[:, :side].astype(jnp.bfloat16)
            three_ref[2 * g + 1, here, :LANES] = jnp.where(left, high_turned, low).astype(jnp.bfloat16)
            three_ref[2 * g + 1, here, LANES:] = high_turned[:, :side].astype(jnp.bfloat16)


def prepare(place, names, amplitudes, n_blocks):
    rows, width = amplitudes.shape
    slots = names.shape[1]
    side = width // slots
    return pl.pallas_call(
        functools.partial(prepare_kernel, n_blocks, side),
        out_shape=[
            pltpu.VMEM((slots, rows, 3 * side), jnp.bfloat16),
            pltpu.VMEM((slots, LANES), jnp.int32),
        ],
        in_specs=[SMEM, HBM, HBM],
        out_specs=[VMEM, VMEM],
        scratch_shapes=[
            pltpu.SMEM((1, slots), jnp.int32),
            pltpu.VMEM((n_blocks, rows // n_blocks, width), jnp.float32),
            pltpu.SemaphoreType.DMA((n_blocks + 1,)),
        ],
        compiler_params=PARAMS,
        name="prepare",
        cost_estimate=pl.CostEstimate(flops=100, bytes_accessed=100, transcendentals=0),
    )(place, in_hbm(names), in_hbm(amplitudes))


def product_kernel(n_in, n_outs, first, side, count, names_ref, three_ref, *refs):
    packs = refs[:n_in]
    outs = refs[-n_outs:]
    words = []
    rows = count // 2 * side + 8
    parts = [(pack, base) for pack in packs for base in range(0, pack.shape[0], rows)]
    slots = names_ref.shape[0]
    slot_id = lax.broadcasted_iota(jnp.int32, (slots, LANES), 0) + 1
    for j, (pack, base) in enumerate(parts):
        row = pack[base + rows - 8 : base + rows - 7, :].astype(jnp.int32)
        slot = jnp.sum(jnp.where(names_ref[...] == row, slot_id, 0), axis=0, keepdims=True)
        col = pack[base + rows - 7 : base + rows - 6, :].astype(jnp.int32)
        words.append(slot * AB_TILES + col)
    if first:
        for out_ref in outs:
            out_ref[...] = jnp.zeros_like(out_ref)

    lane = lax.broadcasted_iota(jnp.int32, (1, LANES), 1)
    tiles = [(j, t) for j in range(len(parts)) for t in range(count)]
    for start in range(0, len(tiles), UNROLL):
        products = []
        for j, t in tiles[start : start + UNROLL]:
            word = words[j][0, t]
            col = word & (AB_TILES - 1)
            slot = word // AB_TILES
            goal = col & 1
            pack, base = parts[j]
            pair = pack[base + t // 2 * side : base + (t // 2 + 1) * side, :]
            turned = jnp.where(goal == t % 2, pair, pltpu.roll(pair, side, 1))
            keep = (lane >= goal * side) & (lane < goal * side + side) & (slot > 0)
            high, low = split(jnp.where(keep, turned, 0.0))
            weights = jnp.concatenate([high, high, low], axis=0)
            values = three_ref[jnp.maximum(slot - 1, 0)]
            products.append(
                (
                    pl.multiple_of(col // 2 * LANES, LANES),
                    jnp.dot(values, weights, preferred_element_type=jnp.float32),
                )
            )
        for column, product in products:
            top = 0
            for out_ref in outs:
                height = out_ref.shape[0]
                out_ref[:, pl.ds(column, LANES)] += product[top : top + height]
                top += height


def accumulate(names, three, packs, totals, heights, side, count):
    n_in = len(packs)
    blocks = [pltpu.VMEM((height, AB_TILES * side), jnp.float32) for height in heights]
    carried = [] if totals is None else [in_vmem(total) for total in totals]
    return pl.pallas_call(
        functools.partial(product_kernel, n_in, len(heights), totals is None, side, count),
        out_shape=blocks,
        in_specs=[VMEM] * (2 + n_in + len(carried)),
        out_specs=[VMEM] * len(heights),
        input_output_aliases={2 + n_in + b: b for b in range(len(carried))},
        compiler_params=PARAMS,
        name="products",
        cost_estimate=pl.CostEstimate(flops=100, bytes_accessed=100, transcendentals=0),
    )(in_vmem(names), in_vmem(three), *map(in_vmem, packs), *carried)


def add_kernel(carried_ref, more_ref, out_ref):
    out_ref[...] = carried_ref[...] + more_ref[...]


def added(carried, more):
    return pl.pallas_call(
        add_kernel,
        out_shape=pltpu.VMEM(carried.shape, carried.dtype),
        in_specs=[VMEM, VMEM],
        out_specs=VMEM,
        input_output_aliases={0: 0},
        compiler_params=PARAMS,
        name="added",
        cost_estimate=pl.CostEstimate(flops=0, bytes_accessed=8 << 20, transcendentals=0),
    )(in_vmem(carried), in_vmem(more))


def local(n_occ, n_vir, amplitudes, amp_cols, integrals, int_rows, int_cols):
    side, width = integrals.shape[2:]
    count = width // side
    place = lax.axis_index("vir").astype(jnp.int32).reshape(1)

    def swap(value, mask):
        return lax.ppermute(value, "occ", [(i, i ^ mask) for i in range(n_occ)])

    def along(value, mask):
        return lax.ppermute(value, "vir", [(i, i ^ mask) for i in range(n_vir)])

    own = pack(
        integrals.reshape(side, width),
        int_rows.reshape(1, count),
        int_cols.reshape(1, count),
    )
    height = amplitudes.shape[0] // n_vir
    pieces = [2] * n_vir
    heights = [height // pieces[r] for r in range(n_vir) for _ in range(pieces[r])]

    def add(packs, blocks):
        return accumulate(names, three, packs, blocks, heights, side, count // PARTS)

    if n_occ == 8:
        x, y, far, close = (swap(own, mask) for mask in (2, 4, 6, 1))
        three, names = prepare(place, amp_cols, amplitudes, n_vir)
        blocks = add([own], None)
        x, y, blocks = together(x, y, blocks)
        x_turned, y_turned = swap(x, 1), swap(y, 1)
        blocks = add([x, y, close], blocks)
        far, blocks = together(far, blocks)
        far_turned = swap(far, 1)
        blocks = add([x_turned, y_turned, far], blocks)
        blocks = add([far_turned], blocks)
    else:
        three, names = prepare(place, amp_cols, amplitudes, n_vir)
        blocks = add([own], None)
        for mask in range(1, n_occ):
            blocks = add([swap(own, mask)], blocks)

    blocks = iter(blocks)
    blocks = [[next(blocks) for _ in range(pieces[r])] for r in range(n_vir)]
    bit = 1
    while bit < n_vir:
        for r in range(n_vir - bit, 1, -2 * bit):
            got = [along(piece, bit) for piece in blocks[r]]
            goal = blocks[r ^ bit]
            goal[0] = added(goal[0], got[0])
            if r == 2:
                upper = along(blocks[1][0], 1)
                upper, goal[0], goal[1] = together(upper, goal[0], goal[1])
            goal[1] = added(goal[1], got[1])
        if bit == 1:
            blocks[2][0], *blocks[1] = together(blocks[2][0], *blocks[1])
        bit *= 2
    lower = along(blocks[1][1], 1)
    return jnp.concatenate(blocks[0], axis=0) + jnp.concatenate([upper, lower], axis=0)


def solution(mesh):
    return jax.shard_map(
        functools.partial(local, mesh.shape["occ"], mesh.shape["vir"]),
        mesh=mesh,
        in_specs=(
            P("occ", None),
            P("occ", None),
            P("vir", "occ", None, None),
            P("vir", "occ", None),
            P("vir", "occ", None),
        ),
        out_specs=P(("occ", "vir"), None),
        check_vma=False,
    )
```

```python
import functools

import jax
import jax.numpy as jnp
from jax import lax
from jax.experimental import pallas as pl
from jax.experimental.pallas import tpu as pltpu
from jax.sharding import PartitionSpec as P

AB_TILES = 32
LANES = 128
UNROLL = 8
PARTS = 1
HBM = pl.BlockSpec(memory_space=pltpu.HBM)
SMEM = pl.BlockSpec(memory_space=pltpu.SMEM)
VMEM = pl.BlockSpec(memory_space=pltpu.VMEM)
PARAMS = pltpu.CompilerParams(vmem_limit_bytes=8 * 1024 * 1024)


def in_vmem(value):
    return pltpu.with_memory_space_constraint(value, pltpu.VMEM)


def in_hbm(value):
    return pltpu.with_memory_space_constraint(value, pltpu.HBM)


def together(*values):
    return lax.optimization_barrier(values)


def pack_kernel(tiles_ref, rows_ref, cols_ref, out_ref, numbers, sems):
    side, width = tiles_ref.shape
    count = rows_ref.shape[1] // PARTS
    groups = width // LANES // PARTS
    rows = groups * side + 8
    copies = [
        pltpu.make_async_copy(rows_ref, numbers.at[0], sems.at[0]),
        pltpu.make_async_copy(cols_ref, numbers.at[1], sems.at[1]),
    ]
    for n in range(PARTS * groups):
        copies.append(
            pltpu.make_async_copy(
                tiles_ref.at[:, pl.ds(n * LANES, LANES)],
                out_ref.at[pl.ds(n // groups * rows + n % groups * side, side)],
                sems.at[2 + n],
            )
        )
    for copy in copies:
        copy.start()
    for p in range(PARTS):
        out_ref[(p + 1) * rows - 8 : (p + 1) * rows, :] = jnp.zeros((8, LANES), jnp.float32)
    for copy in copies[:2]:
        copy.wait()
    for p in range(PARTS):
        for k in range(2):
            place = (p + 1) * rows - 8 + k
            values = numbers[k][:, p * count : (p + 1) * count]
            out_ref[place : place + 1, :count] = values.astype(jnp.float32)
    for copy in copies[2:]:
        copy.wait()


def pack(tiles, rows, cols):
    side, width = tiles.shape
    groups = width // LANES
    return pl.pallas_call(
        pack_kernel,
        out_shape=pltpu.VMEM((groups * side + PARTS * 8, LANES), jnp.float32),
        in_specs=[HBM] * 3,
        out_specs=VMEM,
        scratch_shapes=[
            pltpu.VMEM((2, 1, rows.shape[1]), jnp.int32),
            pltpu.SemaphoreType.DMA((2 + groups,)),
        ],
        compiler_params=PARAMS,
        name="pack",
    )(in_hbm(tiles), in_hbm(rows), in_hbm(cols))


def split(value):
    high = value.astype(jnp.bfloat16)
    low = (value - high.astype(jnp.float32)).astype(jnp.bfloat16)
    return high, low


def prepare_kernel(n_blocks, side, place_ref, names_in, amp_ref, three_ref, names_out, names_ref, amps, sems):
    place = place_ref[0]
    rows = amp_ref.shape[0]
    height = rows // n_blocks
    names_copy = pltpu.make_async_copy(names_in, names_ref, sems.at[n_blocks])
    names_copy.start()
    copies = []
    for b in range(n_blocks):
        source = pl.ds(pl.multiple_of((place ^ b) * height, height), height)
        copy = pltpu.make_async_copy(amp_ref.at[source], amps.at[b], sems.at[b])
        copy.start()
        copies.append(copy)
    names_copy.wait()
    for s in range(names_ref.shape[1]):
        names_out[s : s + 1, :] = jnp.full((1, LANES), names_ref[0, s], jnp.int32)
    lane = lax.broadcasted_iota(jnp.int32, (1, LANES), 1)
    left = lane < side
    for b in range(n_blocks):
        here = slice(b * height, (b + 1) * height)
        copies[b].wait()
        for g in range(amp_ref.shape[1] // LANES):
            both = amps[b, :, g * LANES : (g + 1) * LANES]
            high = both.astype(jnp.bfloat16).astype(jnp.float32)
            low = both - high
            high_turned = pltpu.roll(high, side, 1)
            low_turned = pltpu.roll(low, side, 1)
            three_ref[2 * g, here, :LANES] = jnp.where(left, high, low_turned).astype(jnp.bfloat16)
            three_ref[2 * g, here, LANES:] = high[:, :side].astype(jnp.bfloat16)
            three_ref[2 * g + 1, here, :LANES] = jnp.where(left, high_turned, low).astype(jnp.bfloat16)
            three_ref[2 * g + 1, here, LANES:] = high_turned[:, :side].astype(jnp.bfloat16)


def prepare(place, names, amplitudes, n_blocks):
    rows, width = amplitudes.shape
    slots = names.shape[1]
    side = width // slots
    return pl.pallas_call(
        functools.partial(prepare_kernel, n_blocks, side),
        out_shape=[
            pltpu.VMEM((slots, rows, 3 * side), jnp.bfloat16),
            pltpu.VMEM((slots, LANES), jnp.int32),
        ],
        in_specs=[SMEM, HBM, HBM],
        out_specs=[VMEM, VMEM],
        scratch_shapes=[
            pltpu.SMEM((1, slots), jnp.int32),
            pltpu.VMEM((n_blocks, rows // n_blocks, width), jnp.float32),
            pltpu.SemaphoreType.DMA((n_blocks + 1,)),
        ],
        compiler_params=PARAMS,
        name="prepare",
        cost_estimate=pl.CostEstimate(flops=100, bytes_accessed=100, transcendentals=0),
    )(place, in_hbm(names), in_hbm(amplitudes))


def product_kernel(n_in, n_outs, first, side, count, names_ref, three_ref, *refs):
    packs = refs[:n_in]
    outs = refs[-n_outs:]
    words = []
    rows = count // 2 * side + 8
    parts = [(pack, base) for pack in packs for base in range(0, pack.shape[0], rows)]
    slots = names_ref.shape[0]
    slot_id = lax.broadcasted_iota(jnp.int32, (slots, LANES), 0) + 1
    for j, (pack, base) in enumerate(parts):
        row = pack[base + rows - 8 : base + rows - 7, :].astype(jnp.int32)
        slot = jnp.sum(jnp.where(names_ref[...] == row, slot_id, 0), axis=0, keepdims=True)
        col = pack[base + rows - 7 : base + rows - 6, :].astype(jnp.int32)
        words.append(slot * AB_TILES + col)
    if first:
        for out_ref in outs:
            out_ref[...] = jnp.zeros_like(out_ref)

    lane = lax.broadcasted_iota(jnp.int32, (1, LANES), 1)
    tiles = [(j, t) for j in range(len(parts)) for t in range(count)]
    for start in range(0, len(tiles), UNROLL):
        products = []
        for j, t in tiles[start : start + UNROLL]:
            word = words[j][0, t]
            col = word & (AB_TILES - 1)
            slot = word // AB_TILES
            goal = col & 1
            pack, base = parts[j]
            pair = pack[base + t // 2 * side : base + (t // 2 + 1) * side, :]
            turned = jnp.where(goal == t % 2, pair, pltpu.roll(pair, side, 1))
            keep = (lane >= goal * side) & (lane < goal * side + side) & (slot > 0)
            high, low = split(jnp.where(keep, turned, 0.0))
            weights = jnp.concatenate([high, high, low], axis=0)
            values = three_ref[jnp.maximum(slot - 1, 0)]
            products.append(
                (
                    pl.multiple_of(col // 2 * LANES, LANES),
                    jnp.dot(values, weights, preferred_element_type=jnp.float32),
                )
            )
        for column, product in products:
            top = 0
            for out_ref in outs:
                height = out_ref.shape[0]
                out_ref[:, pl.ds(column, LANES)] += product[top : top + height]
                top += height


def accumulate(names, three, packs, totals, heights, side, count):
    n_in = len(packs)
    blocks = [pltpu.VMEM((height, AB_TILES * side), jnp.float32) for height in heights]
    carried = [] if totals is None else [in_vmem(total) for total in totals]
    return pl.pallas_call(
        functools.partial(product_kernel, n_in, len(heights), totals is None, side, count),
        out_shape=blocks,
        in_specs=[VMEM] * (2 + n_in + len(carried)),
        out_specs=[VMEM] * len(heights),
        input_output_aliases={2 + n_in + b: b for b in range(len(carried))},
        compiler_params=PARAMS,
        name="products",
        cost_estimate=pl.CostEstimate(flops=100, bytes_accessed=100, transcendentals=0),
    )(in_vmem(names), in_vmem(three), *map(in_vmem, packs), *carried)


def add_kernel(carried_ref, more_ref, out_ref):
    out_ref[...] = carried_ref[...] + more_ref[...]


def added(carried, more):
    return pl.pallas_call(
        add_kernel,
        out_shape=pltpu.VMEM(carried.shape, carried.dtype),
        in_specs=[VMEM, VMEM],
        out_specs=VMEM,
        input_output_aliases={0: 0},
        compiler_params=PARAMS,
        name="added",
        cost_estimate=pl.CostEstimate(flops=0, bytes_accessed=8 << 20, transcendentals=0),
    )(in_vmem(carried), in_vmem(more))


def mix_kernel(flag_ref, far_ref, more_ref, near_ref, first_ref, second_ref):
    total = far_ref[...] + more_ref[...]
    near = near_ref[...]
    inner = flag_ref[0] > 0
    first_ref[...] = jnp.where(inner, total, near)
    second_ref[...] = jnp.where(inner, near, total)


def mixed(flag, far, more, near):
    block = pltpu.VMEM(far.shape, far.dtype)
    return pl.pallas_call(
        mix_kernel,
        out_shape=[block, block],
        in_specs=[SMEM, VMEM, VMEM, VMEM],
        out_specs=[VMEM, VMEM],
        compiler_params=PARAMS,
        name="mixed",
    )(flag, in_vmem(far), in_vmem(more), in_vmem(near))


def local(n_occ, n_vir, amplitudes, amp_cols, integrals, int_rows, int_cols):
    side, width = integrals.shape[2:]
    count = width // side
    place = lax.axis_index("vir").astype(jnp.int32).reshape(1)

    def swap(value, mask):
        return lax.ppermute(value, "occ", [(i, i ^ mask) for i in range(n_occ)])

    def along(value, mask):
        return lax.ppermute(value, "vir", [(i, i ^ mask) for i in range(n_vir)])

    own = pack(
        integrals.reshape(side, width),
        int_rows.reshape(1, count),
        int_cols.reshape(1, count),
    )
    height = amplitudes.shape[0] // n_vir
    pieces = [2] * n_vir
    heights = [height // pieces[r] for r in range(n_vir) for _ in range(pieces[r])]

    def add(packs, blocks):
        return accumulate(names, three, packs, blocks, heights, side, count // PARTS)

    if n_occ == 8:
        x, y, far, close = (swap(own, mask) for mask in (2, 4, 6, 1))
        three, names = prepare(place, amp_cols, amplitudes, n_vir)
        blocks = add([own], None)
        x, y, blocks = together(x, y, blocks)
        x_turned, y_turned = swap(x, 1), swap(y, 1)
        blocks = add([x, y, close], blocks)
        far, blocks = together(far, blocks)
        far_turned = swap(far, 1)
        blocks = add([x_turned, y_turned, far], blocks)
        blocks = add([far_turned], blocks)
    else:
        three, names = prepare(place, amp_cols, amplitudes, n_vir)
        blocks = add([own], None)
        for mask in range(1, n_occ):
            blocks = add([swap(own, mask)], blocks)

    blocks = iter(blocks)
    blocks = [[next(blocks) for _ in range(pieces[r])] for r in range(n_vir)]
    if n_vir == 4:
        mine, near, away, far = blocks
        inner = ((place + 1) // 2 == 1).astype(jnp.int32)
        rings = [(0, 1), (1, 3), (2, 0), (3, 2)], [(0, 2), (1, 0), (2, 3), (3, 1)]
        come = [along(piece, 1) for piece in far]
        sent = [mixed(inner, *group) for group in zip(away, come, near)]
        got = [[lax.ppermute(piece, "vir", ring) for piece, ring in zip(pair, rings)] for pair in sent]
        upper = added(added(mine[0], got[0][0]), got[0][1])
        upper, mine[1] = together(upper, mine[1])
        return jnp.concatenate([upper, added(mine[1], got[1][0]) + got[1][1]], axis=0)
    bit = 1
    while bit < n_vir:
        for r in range(n_vir - bit, 0, -2 * bit):
            got = [along(piece, bit) for piece in blocks[r]]
            blocks[r ^ bit] = [added(old, new) for old, new in zip(blocks[r ^ bit], got)]
        bit *= 2
    return jnp.concatenate(blocks[0], axis=0)


def solution(mesh):
    return jax.shard_map(
        functools.partial(local, mesh.shape["occ"], mesh.shape["vir"]),
        mesh=mesh,
        in_specs=(
            P("occ", None),
            P("occ", None),
            P("vir", "occ", None, None),
            P("vir", "occ", None),
            P("vir", "occ", None),
        ),
        out_specs=P(("occ", "vir"), None),
        check_vma=False,
    )
```

```python
import functools

import jax
import jax.numpy as jnp
from jax import lax
from jax.experimental import pallas as pl
from jax.experimental.pallas import tpu as pltpu
from jax.sharding import PartitionSpec as P

AB_TILES = 32
LANES = 128
UNROLL = 8
PARTS = 2
HBM = pl.BlockSpec(memory_space=pltpu.HBM)
SMEM = pl.BlockSpec(memory_space=pltpu.SMEM)
VMEM = pl.BlockSpec(memory_space=pltpu.VMEM)
PARAMS = pltpu.CompilerParams(vmem_limit_bytes=8 * 1024 * 1024)


def in_vmem(value):
    return pltpu.with_memory_space_constraint(value, pltpu.VMEM)


def in_hbm(value):
    return pltpu.with_memory_space_constraint(value, pltpu.HBM)


def together(*values):
    return lax.optimization_barrier(values)


def pack_kernel(tiles_ref, rows_ref, cols_ref, *refs):
    outs, numbers, sems = refs[:-2], refs[-2], refs[-1]
    side, width = tiles_ref.shape
    count = rows_ref.shape[1] // len(outs)
    groups = width // LANES // len(outs)
    base = groups * side
    copies = [
        pltpu.make_async_copy(rows_ref, numbers.at[0], sems.at[0]),
        pltpu.make_async_copy(cols_ref, numbers.at[1], sems.at[1]),
    ]
    for p, out_ref in enumerate(outs):
        for g in range(groups):
            n = p * groups + g
            copies.append(
                pltpu.make_async_copy(
                    tiles_ref.at[:, pl.ds(n * LANES, LANES)],
                    out_ref.at[pl.ds(g * side, side)],
                    sems.at[2 + n],
                )
            )
    for copy in copies:
        copy.start()
    for out_ref in outs:
        out_ref[base : base + 8, :] = jnp.zeros((8, LANES), jnp.float32)
    for copy in copies[:2]:
        copy.wait()
    for p, out_ref in enumerate(outs):
        for k in range(2):
            values = numbers[k][:, p * count : (p + 1) * count]
            out_ref[base + k : base + k + 1, :count] = values.astype(jnp.float32)
    for copy in copies[2:]:
        copy.wait()


def pack(tiles, rows, cols, parts):
    side, width = tiles.shape
    groups = width // LANES
    return pl.pallas_call(
        pack_kernel,
        out_shape=[pltpu.VMEM((groups // parts * side + 8, LANES), jnp.float32)] * parts,
        in_specs=[HBM] * 3,
        out_specs=[VMEM] * parts,
        scratch_shapes=[
            pltpu.VMEM((2, 1, rows.shape[1]), jnp.int32),
            pltpu.SemaphoreType.DMA((2 + groups,)),
        ],
        compiler_params=PARAMS,
        name="pack",
    )(in_hbm(tiles), in_hbm(rows), in_hbm(cols))


def split(value):
    high = value.astype(jnp.bfloat16)
    low = (value - high.astype(jnp.float32)).astype(jnp.bfloat16)
    return high, low


def prepare_kernel(n_blocks, side, place_ref, names_in, amp_ref, three_ref, names_out, names_ref, amps, sems):
    place = place_ref[0]
    rows = amp_ref.shape[0]
    height = rows // n_blocks
    names_copy = pltpu.make_async_copy(names_in, names_ref, sems.at[n_blocks])
    names_copy.start()
    copies = []
    for b in range(n_blocks):
        source = pl.ds(pl.multiple_of((place ^ b) * height, height), height)
        copy = pltpu.make_async_copy(amp_ref.at[source], amps.at[b], sems.at[b])
        copy.start()
        copies.append(copy)
    names_copy.wait()
    for s in range(names_ref.shape[1]):
        names_out[s : s + 1, :] = jnp.full((1, LANES), names_ref[0, s], jnp.int32)
    lane = lax.broadcasted_iota(jnp.int32, (1, LANES), 1)
    left = lane < side
    for b in range(n_blocks):
        here = slice(b * height, (b + 1) * height)
        copies[b].wait()
        for g in range(amp_ref.shape[1] // LANES):
            both = amps[b, :, g * LANES : (g + 1) * LANES]
            high = both.astype(jnp.bfloat16).astype(jnp.float32)
            low = both - high
            high_turned = pltpu.roll(high, side, 1)
            low_turned = pltpu.roll(low, side, 1)
            three_ref[2 * g, here, :LANES] = jnp.where(left, high, low_turned).astype(jnp.bfloat16)
            three_ref[2 * g, here, LANES:] = high[:, :side].astype(jnp.bfloat16)
            three_ref[2 * g + 1, here, :LANES] = jnp.where(left, high_turned, low).astype(jnp.bfloat16)
            three_ref[2 * g + 1, here, LANES:] = high_turned[:, :side].astype(jnp.bfloat16)


def prepare(place, names, amplitudes, n_blocks):
    rows, width = amplitudes.shape
    slots = names.shape[1]
    side = width // slots
    return pl.pallas_call(
        functools.partial(prepare_kernel, n_blocks, side),
        out_shape=[
            pltpu.VMEM((slots, rows, 3 * side), jnp.bfloat16),
            pltpu.VMEM((slots, LANES), jnp.int32),
        ],
        in_specs=[SMEM, HBM, HBM],
        out_specs=[VMEM, VMEM],
        scratch_shapes=[
            pltpu.SMEM((1, slots), jnp.int32),
            pltpu.VMEM((n_blocks, rows // n_blocks, width), jnp.float32),
            pltpu.SemaphoreType.DMA((n_blocks + 1,)),
        ],
        compiler_params=PARAMS,
        name="prepare",
        cost_estimate=pl.CostEstimate(flops=100, bytes_accessed=100, transcendentals=0),
    )(place, in_hbm(names), in_hbm(amplitudes))


def product_kernel(n_in, n_outs, first, side, count, names_ref, three_ref, *refs):
    packs = refs[:n_in]
    outs = refs[-n_outs:]
    words = []
    rows = count // 2 * side + 8
    parts = [(pack, base) for pack in packs for base in range(0, pack.shape[0], rows)]
    slots = names_ref.shape[0]
    slot_id = lax.broadcasted_iota(jnp.int32, (slots, LANES), 0) + 1
    for j, (pack, base) in enumerate(parts):
        row = pack[base + rows - 8 : base + rows - 7, :].astype(jnp.int32)
        slot = jnp.sum(jnp.where(names_ref[...] == row, slot_id, 0), axis=0, keepdims=True)
        col = pack[base + rows - 7 : base + rows - 6, :].astype(jnp.int32)
        words.append(slot * AB_TILES + col)
    if first:
        for out_ref in outs:
            out_ref[...] = jnp.zeros_like(out_ref)

    lane = lax.broadcasted_iota(jnp.int32, (1, LANES), 1)
    tiles = [(j, t) for j in range(len(parts)) for t in range(count)]
    for start in range(0, len(tiles), UNROLL):
        products = []
        for j, t in tiles[start : start + UNROLL]:
            word = words[j][0, t]
            col = word & (AB_TILES - 1)
            slot = word // AB_TILES
            goal = col & 1
            pack, base = parts[j]
            pair = pack[base + t // 2 * side : base + (t // 2 + 1) * side, :]
            turned = jnp.where(goal == t % 2, pair, pltpu.roll(pair, side, 1))
            keep = (lane >= goal * side) & (lane < goal * side + side) & (slot > 0)
            high, low = split(jnp.where(keep, turned, 0.0))
            weights = jnp.concatenate([high, high, low], axis=0)
            values = three_ref[jnp.maximum(slot - 1, 0)]
            products.append(
                (
                    pl.multiple_of(col // 2 * LANES, LANES),
                    jnp.dot(values, weights, preferred_element_type=jnp.float32),
                )
            )
        for column, product in products:
            top = 0
            for out_ref in outs:
                height = out_ref.shape[0]
                out_ref[:, pl.ds(column, LANES)] += product[top : top + height]
                top += height


def accumulate(names, three, packs, totals, heights, side, count):
    n_in = len(packs)
    blocks = [pltpu.VMEM((height, AB_TILES * side), jnp.float32) for height in heights]
    carried = [] if totals is None else [in_vmem(total) for total in totals]
    return pl.pallas_call(
        functools.partial(product_kernel, n_in, len(heights), totals is None, side, count),
        out_shape=blocks,
        in_specs=[VMEM] * (2 + n_in + len(carried)),
        out_specs=[VMEM] * len(heights),
        input_output_aliases={2 + n_in + b: b for b in range(len(carried))},
        compiler_params=PARAMS,
        name="products",
        cost_estimate=pl.CostEstimate(flops=100, bytes_accessed=100, transcendentals=0),
    )(in_vmem(names), in_vmem(three), *map(in_vmem, packs), *carried)


def add_kernel(carried_ref, more_ref, out_ref):
    out_ref[...] = carried_ref[...] + more_ref[...]


def added(carried, more):
    return pl.pallas_call(
        add_kernel,
        out_shape=pltpu.VMEM(carried.shape, carried.dtype),
        in_specs=[VMEM, VMEM],
        out_specs=VMEM,
        input_output_aliases={0: 0},
        compiler_params=PARAMS,
        name="added",
        cost_estimate=pl.CostEstimate(flops=0, bytes_accessed=8 << 20, transcendentals=0),
    )(in_vmem(carried), in_vmem(more))


def mix_kernel(flag_ref, far_ref, more_ref, near_ref, first_ref, second_ref):
    total = far_ref[...] + more_ref[...]
    near = near_ref[...]
    inner = flag_ref[0] > 0
    first_ref[...] = jnp.where(inner, total, near)
    second_ref[...] = jnp.where(inner, near, total)


def mixed(flag, far, more, near):
    block = pltpu.VMEM(far.shape, far.dtype)
    return pl.pallas_call(
        mix_kernel,
        out_shape=[block, block],
        in_specs=[SMEM, VMEM, VMEM, VMEM],
        out_specs=[VMEM, VMEM],
        compiler_params=PARAMS,
        name="mixed",
    )(flag, in_vmem(far), in_vmem(more), in_vmem(near))


def local(n_occ, n_vir, amplitudes, amp_cols, integrals, int_rows, int_cols):
    side, width = integrals.shape[2:]
    count = width // side
    place = lax.axis_index("vir").astype(jnp.int32).reshape(1)

    def swap(value, mask):
        return lax.ppermute(value, "occ", [(i, i ^ mask) for i in range(n_occ)])

    def along(value, mask):
        return lax.ppermute(value, "vir", [(i, i ^ mask) for i in range(n_vir)])

    low, high = pack(
        integrals.reshape(side, width),
        int_rows.reshape(1, count),
        int_cols.reshape(1, count),
        PARTS,
    )
    height = amplitudes.shape[0] // n_vir
    pieces = [2] * n_vir
    heights = [height // pieces[r] for r in range(n_vir) for _ in range(pieces[r])]

    def add(packs, blocks):
        return accumulate(names, three, packs, blocks, heights, side, count // PARTS)

    if n_occ == 8:
        x_low, y_high, x_high, y_low = swap(low, 2), swap(high, 4), swap(high, 2), swap(low, 4)
        close = [swap(low, 1), swap(high, 1)]
        three, names = prepare(place, amp_cols, amplitudes, n_vir)
        blocks = add([low, high], None)
        x_low, y_high, blocks = together(x_low, y_high, blocks)
        far = [swap(x_low, 4), swap(y_high, 2)]
        direct = [x_low, y_high, x_high, y_low]
        blocks = add(direct, blocks)
        x_low, y_high, x_high, y_low, blocks = together(*direct, blocks)
        turned = [swap(value, 1) for value in (x_low, y_high, x_high, y_low)]
        blocks = add(close, blocks)
        *far, blocks = together(*far, blocks)
        last = [swap(value, 1) for value in far]
        blocks = add([*turned, *far], blocks)
        blocks = add(last, blocks)
    else:
        three, names = prepare(place, amp_cols, amplitudes, n_vir)
        blocks = add([low, high], None)
        for mask in range(1, n_occ):
            blocks = add([swap(low, mask), swap(high, mask)], blocks)

    blocks = iter(blocks)
    blocks = [[next(blocks) for _ in range(pieces[r])] for r in range(n_vir)]
    if n_vir == 4:
        mine, near, away, far = blocks
        inner = ((place + 1) // 2 == 1).astype(jnp.int32)
        rings = [(0, 1), (1, 3), (2, 0), (3, 2)], [(0, 2), (1, 0), (2, 3), (3, 1)]
        come = [along(piece, 1) for piece in far]
        sent = [mixed(inner, *group) for group in zip(away, come, near)]
        got = [[lax.ppermute(piece, "vir", ring) for piece, ring in zip(pair, rings)] for pair in sent]
        upper = added(added(mine[0], got[0][0]), got[0][1])
        upper, mine[1] = together(upper, mine[1])
        return jnp.concatenate([upper, added(mine[1], got[1][0]) + got[1][1]], axis=0)
    bit = 1
    while bit < n_vir:
        for r in range(n_vir - bit, 0, -2 * bit):
            got = [along(piece, bit) for piece in blocks[r]]
            blocks[r ^ bit] = [added(old, new) for old, new in zip(blocks[r ^ bit], got)]
        bit *= 2
    return jnp.concatenate(blocks[0], axis=0)


def solution(mesh):
    return jax.shard_map(
        functools.partial(local, mesh.shape["occ"], mesh.shape["vir"]),
        mesh=mesh,
        in_specs=(
            P("occ", None),
            P("occ", None),
            P("vir", "occ", None, None),
            P("vir", "occ", None),
            P("vir", "occ", None),
        ),
        out_specs=P(("occ", "vir"), None),
        check_vma=False,
    )
```
